256 devices in a mesh: section: 8 (over y_lo, x), tp: 32 (over y_hi, z, core).
Axes of the slice: x: 4, y: 4 (y_hi: 2, y_lo: 2; y = y_hi * 2 + y_lo), z: 8, core: 2. Of those that a mesh axis runs over, the one named last changes fastest.
Arguments:
- activations: bfloat16 [8, 512, 4096], P('section', 'tp'), may hold values from -6 to 6
- gate_weight: bfloat16 [8, 4096, 16384], P('section', None, 'tp'), may hold values from -0.09375 to 0.09375
- up_weight: bfloat16 [8, 4096, 16384], P('section', None, 'tp'), may hold values from -0.09375 to 0.09375
- down_weight: bfloat16 [8, 16384, 4096], P('section', 'tp'), may hold values from -0.046875 to 0.046875
- norm_gain: float32 [8, 4096], P('section'), may hold values from 0.5 to 1.5
Outputs:
- passed_on: bfloat16 [8, 512, 4096], P('section', 'tp')
The draws below stay inside these ranges and needn't reach their ends.
All inputs are finite; a program needn't handle non-finite values.
Results may differ from the reference program's by a relative error of at most 0.022.
Values may be sent and summed in bfloat16 or wider, within the bound.
No kernel may reach another device: no remote copies, remote signals or barrier semaphores. Data moves between devices by JAX's collectives and lax.ppermute only.
A program may use at most 64 MiB of HBM per device.

```python
import jax
import jax.numpy as jnp
from jax import lax

D = 4096
FF = 16384
TICKS = 2
TG = 512
FL = 512
N_SECTION = 8
N_TP = 32


def steps_of(own_key, extent, split, smallest, top_value):
    def one(dim, blocks):
        draws = jax.random.uniform(jax.random.fold_in(jax.random.fold_in(own_key, 6), dim), (blocks,), jnp.float32, smallest / len(split), top_value / len(split))
        return jnp.repeat(jnp.exp(draws), extent[dim] // blocks).reshape((-1,) + (1,) * (len(extent) - dim - 1))

    factor_of = one(*split[0])
    for cut in split[1:]:
        factor_of = factor_of * one(*cut)
    return factor_of


def normal_values(stream_key, shape, deviation, most, pieces=(), dtype=jnp.bfloat16):
    factor_of = steps_of(stream_key, shape, pieces, -0.22, 0.18) if pieces else 1.0
    result = jax.random.normal(stream_key, shape, jnp.float32) * deviation * factor_of
    return jnp.minimum(jnp.maximum(result, -most), most).astype(dtype)


def setup_inputs(seed: int = 0) -> dict:
    arg_keys = jax.random.split(jax.random.key(seed), 6)
    activations = normal_values(arg_keys[0], (N_SECTION, TG, D), 1.0, 6.0, ((0, 8), (1, 32)))
    gate_weight = normal_values(arg_keys[1], (N_SECTION, D, FF), D ** -0.5, 0.09375, ((0, 8), (2, 32)))
    up_weight = normal_values(arg_keys[2], (N_SECTION, D, FF), D ** -0.5, 0.09375, ((0, 8), (2, 32)))
    down_weight = normal_values(arg_keys[3], (N_SECTION, FF, D), FF ** -0.5, 0.046875, ((0, 8), (1, 32)))
    norm_gain = jnp.clip(1.0 + 0.1 * jax.random.normal(arg_keys[4], (N_SECTION, D), jnp.float32), 0.5, 1.5)
    return dict(activations=activations, gate_weight=gate_weight, up_weight=up_weight, down_weight=down_weight, norm_gain=norm_gain)


def layer(rows, w_gate, w_up, w_down, gain):
    wide = rows.astype(jnp.float32)
    scale = lax.rsqrt(lax.optimization_barrier(jnp.mean(wide * wide, axis=1, keepdims=True)) + 1e-05)
    normed = (wide * scale * gain[None, :]).astype(jnp.bfloat16)
    gate = jnp.dot(normed, w_gate, preferred_element_type=jnp.float32)
    up = jnp.dot(normed, w_up, preferred_element_type=jnp.float32)
    hidden = (jax.nn.silu(gate) * up).astype(jnp.bfloat16)

    def add_term(index, total):
        start = index.astype(jnp.int32) * FL
        part_h = lax.dynamic_slice_in_dim(hidden, start, FL, 1)
        part_w = lax.dynamic_slice_in_dim(w_down, start, FL, 0)
        term = jnp.dot(part_h, part_w, preferred_element_type=jnp.float32)
        term = lax.optimization_barrier(term.astype(jnp.bfloat16))
        return total + term.astype(jnp.float32)
    branch = lax.fori_loop(0, N_TP, add_term, jnp.zeros((rows.shape[0], rows.shape[1]), jnp.float32))
    return (wide + branch).astype(jnp.bfloat16)

def reference(activations, gate_weight, up_weight, down_weight, norm_gain):
    current = activations
    for tick in range(TICKS):
        results = [layer(current[s], gate_weight[s], up_weight[s], down_weight[s], norm_gain[s]) for s in range(N_SECTION)]
        current = jnp.roll(jnp.stack(results, axis=0), 1, axis=0)
    return current
```

```python
import jax
import jax.numpy as jnp
from jax import lax
from jax.sharding import PartitionSpec as P

TICKS = 2
N_SECTION = 8
N_Y, N_Z, N_CORE = 2, 8, 2
N_TP = N_Y * N_Z * N_CORE
FAR = N_Z // 2


def tp_index(y, z, core):
    return (y * N_Z + z % N_Z) * N_CORE + core


def tp_pairs(target):
    places = [(y, z, c) for y in range(N_Y) for z in range(N_Z) for c in range(N_CORE)]
    return [(tp_index(*place), tp_index(*target(*place))) for place in places]


Z_UP = tp_pairs(lambda y, z, c: (y, z + 1, c))
Z_DOWN = tp_pairs(lambda y, z, c: (y, z - 1, c))
Y_SWAP = tp_pairs(lambda y, z, c: (1 - y, z, c))
CORE_SWAP = tp_pairs(lambda y, z, c: (y, z, 1 - c))
HOP = [(s, (s + 1) % N_SECTION) for s in range(N_SECTION)]
HOP_Y_SWAP = [(s * N_TP + a, t * N_TP + b) for s, t in HOP for a, b in Y_SWAP]


def up(block):
    return lax.ppermute(block, "tp", Z_UP)


def down(block):
    return lax.ppermute(block, "tp", Z_DOWN)


def rms_normed(rows, gain):
    wide = rows.astype(jnp.float32)
    scale = lax.rsqrt(jnp.mean(wide * wide, axis=1, keepdims=True) + 1e-05)
    return (wide * scale * gain[None, :]).astype(jnp.bfloat16)


def dot(a, b):
    return jnp.dot(a, b, preferred_element_type=jnp.float32)


def expand(normed, w_gate, w_up):
    gate = dot(normed, w_gate)
    up_part = dot(normed, w_up)
    return (jax.nn.silu(gate) * up_part).astype(jnp.bfloat16)


def plus(a, b):
    return (a.astype(jnp.float32) + b.astype(jnp.float32)).astype(jnp.bfloat16)


def gathered(own):
    half = own.shape[1] // 2
    blocks = {0: own}
    low = high = own
    for step in range(1, FAR):
        low, high = up(low), down(high)
        blocks[-step], blocks[step] = low, high
    blocks[FAR] = jnp.concatenate([up(low[:, :half]), down(high[:, half:])], axis=1)
    return blocks


def scattered(blocks):
    half = blocks[0].shape[1] // 2
    rise = up(blocks[FAR][:, :half])
    fall = down(blocks[FAR][:, half:])
    above, below = blocks[FAR - 1], blocks[1 - FAR]
    send_up = jnp.concatenate([plus(above[:, :half], rise), above[:, half:]], axis=1)
    send_down = jnp.concatenate([below[:, :half], plus(below[:, half:], fall)], axis=1)
    for step in range(FAR - 2, 0, -1):
        rise, fall = up(send_up), down(send_down)
        send_up, send_down = plus(blocks[step], rise), plus(blocks[-step], fall)
    rise, fall = up(send_up), down(send_down)
    return (blocks[0].astype(jnp.float32) + rise.astype(jnp.float32) + fall.astype(jnp.float32)).astype(jnp.bfloat16)


CHUNKS = ((0, -1, 1), (-2, 2), (-3, 3, 4))


def feed_forward(blocks, weights):
    parts = {}
    for chunk in CHUNKS:
        rows = jnp.concatenate([blocks[j] for j in chunk], axis=0)
        hidden = [expand(rows, w_gate, w_up) for w_gate, w_up, _ in weights]
        hidden = lax.optimization_barrier(hidden)
        part = sum(dot(h, w_down) for h, (_, _, w_down) in zip(hidden, weights)).astype(jnp.bfloat16)
        count = blocks[0].shape[0]
        for i, j in enumerate(chunk):
            parts[j] = part[i * count:(i + 1) * count]
    return parts


def per_device(activations, gate_weight, up_weight, down_weight, norm_gain):
    own_weights = (gate_weight[0], up_weight[0], down_weight[0])
    other_weights = tuple(lax.ppermute(w, "tp", CORE_SWAP) for w in own_weights)
    weights = (own_weights, other_weights)
    gain = norm_gain[0]
    count = activations.shape[1]
    current = jnp.concatenate([activations[0], lax.ppermute(activations[0], "tp", Y_SWAP)], axis=0)
    for tick in range(TICKS):
        last = tick == TICKS - 1
        moved = lax.ppermute(current[:count] if last else current, "section", HOP)
        total = scattered(feed_forward(gathered(rms_normed(current, gain)), weights))
        if last:
            there = lax.ppermute(total[count:], ("section", "tp"), HOP_Y_SWAP)
            here = lax.ppermute(total[:count], "section", HOP)
        else:
            there = lax.ppermute(total, ("section", "tp"), HOP_Y_SWAP)
            there = jnp.concatenate([there[count:], there[:count]], axis=0)
            here = lax.ppermute(total, "section", HOP)
        summed = here.astype(jnp.float32) + there.astype(jnp.float32)
        current = (moved.astype(jnp.float32) + summed).astype(jnp.bfloat16)
    return current[None]


def solution(mesh):
    return jax.shard_map(
        per_device,
        mesh=mesh,
        in_specs=(
            P("section", "tp", None),
            P("section", None, "tp"),
            P("section", None, "tp"),
            P("section", "tp", None),
            P("section", None),
        ),
        out_specs=P("section", "tp", None),
        check_vma=False,
    )
```

```python
import jax
import jax.numpy as jnp
from jax import lax
from jax.sharding import PartitionSpec as P

TICKS = 2
N_SECTION = 8
N_Y, N_Z, N_CORE = 2, 8, 2
N_TP = N_Y * N_Z * N_CORE
FAR = N_Z // 2


def tp_index(y, z, core):
    return (y * N_Z + z % N_Z) * N_CORE + core


def tp_pairs(target):
    places = [(y, z, c) for y in range(N_Y) for z in range(N_Z) for c in range(N_CORE)]
    return [(tp_index(*place), tp_index(*target(*place))) for place in places]


Z_UP = tp_pairs(lambda y, z, c: (y, z + 1, c))
Z_DOWN = tp_pairs(lambda y, z, c: (y, z - 1, c))
Y_SWAP = tp_pairs(lambda y, z, c: (1 - y, z, c))
PAIR_SWAP = tp_pairs(lambda y, z, c: (1 - y, z + FAR, c))
CORE_SWAP = tp_pairs(lambda y, z, c: (y, z, 1 - c))
HOP = [(s, (s + 1) % N_SECTION) for s in range(N_SECTION)]
HOP_PAIR_SWAP = [(s * N_TP + a, t * N_TP + b) for s, t in HOP for a, b in PAIR_SWAP]


def up(block):
    return lax.ppermute(block, "tp", Z_UP)


def down(block):
    return lax.ppermute(block, "tp", Z_DOWN)


def rms_normed(rows, gain):
    wide = rows.astype(jnp.float32)
    scale = lax.rsqrt(jnp.mean(wide * wide, axis=1, keepdims=True) + 1e-05)
    return (wide * scale * gain[None, :]).astype(jnp.bfloat16)


def dot(a, b):
    return jnp.dot(a, b, preferred_element_type=jnp.float32)


def expand(normed, w_gate, w_up):
    gate = dot(normed, w_gate)
    up_part = dot(normed, w_up)
    return (jax.nn.silu(gate) * up_part).astype(jnp.bfloat16)


def plus(a, b):
    return (a.astype(jnp.float32) + b.astype(jnp.float32)).astype(jnp.bfloat16)


def ring(own, steps, after):
    blocks = {0: own}
    low = high = own
    for step in range(1, steps + 1):
        low, high = up(low), down(high)
        if step == 1:
            low, high, *_ = lax.optimization_barrier((low, high, *after))
        else:
            low, high = lax.optimization_barrier((low, high))
        blocks[-step], blocks[step] = low, high
    return blocks


def gathered(own, after=()):
    far = lax.ppermute(own, "tp", Y_SWAP)
    blocks = ring(own, FAR - 1, after)
    blocks[FAR] = far
    return blocks


def gathered_by_y(own, after=()):
    count, half = own.shape[0] // 2, own.shape[1] // 2
    near = ring(own, FAR - 1, after)
    near[FAR] = jnp.concatenate([up(near[1 - FAR][:, :half]), down(near[FAR - 1][:, half:])], axis=1)
    near[-FAR] = near[FAR]

    def pair(j, k):
        return jnp.concatenate([near[j][:count], near[k][count:]], axis=0)

    blocks = {j: pair(j, j + FAR if j <= 0 else j - FAR) for j in range(1 - FAR, FAR)}
    blocks[FAR] = jnp.concatenate([near[0][count:], near[FAR][:count]], axis=0)
    return blocks


def scattered(blocks):
    far = lax.ppermute(blocks[FAR], "tp", Y_SWAP)
    send_up, send_down = blocks[FAR - 1], blocks[1 - FAR]
    for step in range(FAR - 2, 0, -1):
        rise, fall = up(send_up), down(send_down)
        send_up, send_down = plus(blocks[step], rise), plus(blocks[-step], fall)
    rise, fall = up(send_up), down(send_down)
    near = blocks[0].astype(jnp.float32) + far.astype(jnp.float32)
    return (near + rise.astype(jnp.float32) + fall.astype(jnp.float32)).astype(jnp.bfloat16)


EXPAND_CHUNKS = ((3, -3, 4, 2, -2, 1, -1, 0),)
PROJECT_CHUNKS = ((3, -3), (4, 2, -2, 1, -1, 0))


def feed_forward(blocks, weights):
    count = blocks[0].shape[0]
    hidden = {}
    for chunk in EXPAND_CHUNKS:
        rows = jnp.concatenate([blocks[j] for j in chunk], axis=0)
        units = lax.optimization_barrier([expand(rows, w_gate, w_up) for w_gate, w_up, _ in weights])
        for i, j in enumerate(chunk):
            hidden[j] = [u[i * count:(i + 1) * count] for u in units]
    parts = {}
    for chunk in PROJECT_CHUNKS:
        rows = [jnp.concatenate([hidden[j][k] for j in chunk], axis=0) for k in range(len(weights))]
        part = sum(dot(h, w_down) for h, (_, _, w_down) in zip(rows, weights)).astype(jnp.bfloat16)
        for i, j in enumerate(chunk):
            parts[j] = lax.optimization_barrier(part[i * count:(i + 1) * count])
    return parts


def per_device(activations, gate_weight, up_weight, down_weight, norm_gain):
    own_weights = (gate_weight[0], up_weight[0], down_weight[0])
    other_weights = tuple(lax.ppermute(w, "tp", CORE_SWAP) for w in own_weights)
    weights = (own_weights, other_weights)
    gain = norm_gain[0]
    count = activations.shape[1]
    rows = activations[0]
    normed = rms_normed(rows, gain)
    normed = jnp.concatenate([normed, lax.ppermute(normed, "tp", Y_SWAP)], axis=0)
    for tick in range(TICKS):
        total = scattered(feed_forward(gathered(normed) if tick else gathered_by_y(normed, other_weights[:2]), weights))
        own = (rows.astype(jnp.float32) + total[:count].astype(jnp.float32)).astype(jnp.bfloat16)
        partner = total[count:]
        if tick == TICKS - 1:
            there = lax.ppermute(partner, ("section", "tp"), HOP_PAIR_SWAP)
            here = lax.ppermute(own, "section", HOP)
            return plus(here, there)[None]
        there = lax.ppermute(jnp.concatenate([partner, own], axis=0), ("section", "tp"), HOP_PAIR_SWAP)
        here = lax.ppermute(jnp.concatenate([own, partner], axis=0), "section", HOP)
        both = plus(here, there)
        rows = both[:count]
        normed = rms_normed(both, gain)


def solution(mesh):
    return jax.shard_map(
        per_device,
        mesh=mesh,
        in_specs=(
            P("section", "tp", None),
            P("section", None, "tp"),
            P("section", None, "tp"),
            P("section", "tp", None),
            P("section", None),
        ),
        out_specs=P("section", "tp", None),
        check_vma=False,
    )
```

```python
import jax
import jax.numpy as jnp
from jax import lax
from jax.sharding import PartitionSpec as P

TICKS = 2
N_SECTION = 8
N_Y, N_Z, N_CORE = 2, 8, 2
N_TP = N_Y * N_Z * N_CORE
FAR = N_Z // 2


def tp_index(y, z, core):
    return (y * N_Z + z % N_Z) * N_CORE + core


def tp_pairs(target):
    places = [(y, z, c) for y in range(N_Y) for z in range(N_Z) for c in range(N_CORE)]
    return [(tp_index(*place), tp_index(*target(*place))) for place in places]


Z_UP = tp_pairs(lambda y, z, c: (y, z + 1, c))
Z_DOWN = tp_pairs(lambda y, z, c: (y, z - 1, c))
Y_SWAP = tp_pairs(lambda y, z, c: (1 - y, z, c))
PAIR_SWAP = tp_pairs(lambda y, z, c: (1 - y, z + FAR, c))
CORE_SWAP = tp_pairs(lambda y, z, c: (y, z, 1 - c))
HOP = [(s, (s + 1) % N_SECTION) for s in range(N_SECTION)]
HOP_PAIR_SWAP = [(s * N_TP + a, t * N_TP + b) for s, t in HOP for a, b in PAIR_SWAP]


def up(block):
    return lax.ppermute(block, "tp", Z_UP)


def down(block):
    return lax.ppermute(block, "tp", Z_DOWN)


def rms_normed(rows, gain):
    wide = rows.astype(jnp.float32)
    scale = lax.rsqrt(jnp.mean(wide * wide, axis=1, keepdims=True) + 1e-05)
    return (wide * scale * gain[None, :]).astype(jnp.bfloat16)


def dot(a, b):
    return jnp.dot(a, b, preferred_element_type=jnp.float32)


def expand(normed, w_gate, w_up):
    gate = dot(normed, w_gate)
    up_part = dot(normed, w_up)
    return (jax.nn.silu(gate) * up_part).astype(jnp.bfloat16)


def plus(*terms):
    return sum(term.astype(jnp.float32) for term in terms).astype(jnp.bfloat16)


def stacked(*pieces):
    return jnp.concatenate(pieces, axis=0)


def gathered(own, after):
    count = own.shape[0]
    pieces = {("own", 0): own}
    pair = lax.ppermute(own, "tp", PAIR_SWAP)
    low, high = up(own), down(own)
    here = lax.ppermute(own, "tp", Y_SWAP)
    low, high, pair, here, *_ = lax.optimization_barrier((low, high, pair, here, *after))
    pieces["own", -1], pieces["own", 1], pieces["pair", FAR] = low, high, pair
    near = lax.ppermute(stacked(high, low), "tp", Y_SWAP)
    low, high = up(stacked(low, pair)), down(stacked(high, pair))
    low, high, near = lax.optimization_barrier((low, high, near))
    pieces["pair", 1], pieces["pair", -1] = near[:count], near[count:]
    pieces["own", -2], pieces["pair", 3] = low[:count], low[count:]
    pieces["own", 2], pieces["pair", -3] = high[:count], high[count:]
    pieces["pair", 0], pieces["own", FAR] = here, lax.ppermute(pair, "tp", Y_SWAP)
    low, high = lax.optimization_barrier((up(low), down(high)))
    pieces["own", -3], pieces["pair", 2] = low[:count], low[count:]
    pieces["own", 3], pieces["pair", -2] = high[:count], high[count:]
    return pieces


FIRST = tuple(("own", j) for j in (3, -3, FAR)) + tuple(("pair", j) for j in (2, -2, 1, -1, 0))
REST = tuple(("own", j) for j in (2, -2, 1, -1, 0)) + tuple(("pair", j) for j in (-3, 3, FAR))


def feed_forward(pieces, weights):
    count = pieces[FIRST[0]].shape[0]
    rows = stacked(*(pieces[name] for name in FIRST + REST))
    units = lax.optimization_barrier([expand(rows, w_gate, w_up) for w_gate, w_up, _ in weights])
    parts = {}
    start = 0
    for names in (FIRST, REST):
        stop = start + len(names) * count
        part = sum(dot(u[start:stop], w_down) for u, (_, _, w_down) in zip(units, weights)).astype(jnp.bfloat16)
        for i, name in enumerate(names):
            parts[name] = lax.optimization_barrier(part[i * count:(i + 1) * count])
        start = stop
    return parts


def scattered(parts):
    count = parts["own", 0].shape[0]
    near = stacked(*(parts[name] for name in (("pair", 1), ("pair", -1), ("own", FAR), ("pair", 0))))
    near = lax.ppermute(near, "tp", Y_SWAP)
    send_up = stacked(parts["own", 3], parts["pair", -2])
    send_down = stacked(parts["own", -3], parts["pair", 2])
    rise, fall = lax.optimization_barrier((up(send_up), down(send_down)))
    send_up = stacked(plus(parts["own", 2], rise[:count]), plus(parts["pair", -3], rise[count:]))
    send_down = stacked(plus(parts["own", -2], fall[:count]), plus(parts["pair", 3], fall[count:]))
    rise, fall = lax.optimization_barrier((up(send_up), down(send_down)))
    send_up = plus(parts["own", 1], rise[:count], near[:count])
    send_down = plus(parts["own", -1], fall[:count], near[count:2 * count])
    pair = plus(parts["pair", FAR], rise[count:], fall[count:], near[2 * count:3 * count])
    return (parts["own", 0], near[3 * count:], up(send_up), down(send_down)), pair


def per_device(activations, gate_weight, up_weight, down_weight, norm_gain):
    own_weights = (gate_weight[0], up_weight[0], down_weight[0])
    other_weights = tuple(lax.ppermute(w, "tp", CORE_SWAP) for w in own_weights)
    weights = (own_weights, other_weights)
    gain = norm_gain[0]
    rows = activations[0]
    for tick in range(TICKS):
        pieces = gathered(rms_normed(rows, gain), () if tick else other_weights[:2])
        shares, pair = scattered(feed_forward(pieces, weights))
        there = lax.ppermute(pair, ("section", "tp"), HOP_PAIR_SWAP)
        rows = plus(lax.ppermute(plus(rows, *shares), "section", HOP), there)
    return rows[None]


def solution(mesh):
    return jax.shard_map(
        per_device,
        mesh=mesh,
        in_specs=(
            P("section", "tp", None),
            P("section", None, "tp"),
            P("section", None, "tp"),
            P("section", "tp", None),
            P("section", None),
        ),
        out_specs=P("section", "tp", None),
        check_vma=False,
    )
```

```python
import jax
import jax.numpy as jnp
from jax import lax
from jax.sharding import PartitionSpec as P

TICKS = 2
N_SECTION = 8
N_Y, N_Z, N_CORE = 2, 8, 2
N_TP = N_Y * N_Z * N_CORE
FAR = N_Z // 2


def tp_index(y, z, core):
    return (y * N_Z + z % N_Z) * N_CORE + core


def tp_pairs(target):
    places = [(y, z, c) for y in range(N_Y) for z in range(N_Z) for c in range(N_CORE)]
    return [(tp_index(*place), tp_index(*target(*place))) for place in places]


Z_UP = tp_pairs(lambda y, z, c: (y, z + 1, c))
Z_DOWN = tp_pairs(lambda y, z, c: (y, z - 1, c))
Y_SWAP = tp_pairs(lambda y, z, c: (1 - y, z, c))
PAIR_SWAP = tp_pairs(lambda y, z, c: (1 - y, z + FAR, c))
CORE_SWAP = tp_pairs(lambda y, z, c: (y, z, 1 - c))
HOP = [(s, (s + 1) % N_SECTION) for s in range(N_SECTION)]
HOP_PAIR_SWAP = [(s * N_TP + a, t * N_TP + b) for s, t in HOP for a, b in PAIR_SWAP]


def up(block):
    return lax.ppermute(block, "tp", Z_UP)


def down(block):
    return lax.ppermute(block, "tp", Z_DOWN)


def rms_normed(rows, gain):
    wide = rows.astype(jnp.float32)
    scale = lax.rsqrt(jnp.mean(wide * wide, axis=1, keepdims=True) + 1e-05)
    return (wide * scale * gain[None, :]).astype(jnp.bfloat16)


def dot(a, b):
    return jnp.dot(a, b, preferred_element_type=jnp.float32)


def expand(normed, w_gate, w_up):
    gate = dot(normed, w_gate)
    up_part = dot(normed, w_up)
    return (jax.nn.silu(gate) * up_part).astype(jnp.bfloat16)


def plus(*terms):
    return sum(term.astype(jnp.float32) for term in terms).astype(jnp.bfloat16)


def stacked(*pieces):
    return jnp.concatenate(pieces, axis=0)


def gathered(own, after):
    count = own.shape[0]
    pieces = {("own", 0): own}
    pair = lax.ppermute(own, "tp", PAIR_SWAP)
    here = lax.ppermute(own, "tp", Y_SWAP)
    low, high = up(own), down(own)
    low, high, pair, here, *_ = lax.optimization_barrier((low, high, pair, here, *after))
    pieces["own", -1], pieces["own", 1], pieces["pair", FAR], pieces["pair", 0] = low, high, pair, here
    far = lax.ppermute(pair, "tp", Y_SWAP)
    low, high = up(stacked(low, pair, here)), down(stacked(high, pair, here))
    low, high, pieces["own", FAR] = lax.optimization_barrier((low, high, far))
    pieces["own", -2], pieces["pair", 3], pieces["pair", -1] = low[:count], low[count:2 * count], low[2 * count:]
    pieces["own", 2], pieces["pair", -3], pieces["pair", 1] = high[:count], high[count:2 * count], high[2 * count:]
    low, high = lax.optimization_barrier((up(low[:2 * count]), down(high[:2 * count])))
    pieces["own", -3], pieces["pair", 2] = low[:count], low[count:]
    pieces["own", 3], pieces["pair", -2] = high[:count], high[count:]
    return pieces


FIRST = tuple(("own", j) for j in (3, -3, FAR)) + tuple(("pair", j) for j in (2, -2, 1, -1, 0))
REST = tuple(("own", j) for j in (2, -2, 1, -1, 0)) + tuple(("pair", j) for j in (-3, 3, FAR))


def feed_forward(pieces, weights):
    count = pieces[FIRST[0]].shape[0]
    rows = stacked(*(pieces[name] for name in FIRST + REST))
    units = lax.optimization_barrier([expand(rows, w_gate, w_up) for w_gate, w_up, _ in weights])
    parts = {}
    start = 0
    for names in (FIRST, REST):
        stop = start + len(names) * count
        part = sum(dot(u[start:stop], w_down) for u, (_, _, w_down) in zip(units, weights)).astype(jnp.bfloat16)
        for i, name in enumerate(names):
            parts[name] = lax.optimization_barrier(part[i * count:(i + 1) * count])
        start = stop
    return parts


def scattered(parts):
    count = parts["own", 0].shape[0]
    near = stacked(*(parts[name] for name in (("pair", 1), ("pair", -1), ("own", FAR), ("pair", 0))))
    near = lax.ppermute(near, "tp", Y_SWAP)
    send_up = stacked(parts["own", 3], parts["pair", -2])
    send_down = stacked(parts["own", -3], parts["pair", 2])
    rise, fall = lax.optimization_barrier((up(send_up), down(send_down)))
    send_up = stacked(plus(parts["own", 2], rise[:count]), plus(parts["pair", -3], rise[count:]))
    send_down = stacked(plus(parts["own", -2], fall[:count]), plus(parts["pair", 3], fall[count:]))
    rise, fall = lax.optimization_barrier((up(send_up), down(send_down)))
    send_up = plus(parts["own", 1], rise[:count], near[:count])
    send_down = plus(parts["own", -1], fall[:count], near[count:2 * count])
    pair = plus(parts["pair", FAR], rise[count:], fall[count:], near[2 * count:3 * count])
    return (parts["own", 0], near[3 * count:], up(send_up), down(send_down)), pair


def per_device(activations, gate_weight, up_weight, down_weight, norm_gain):
    own_weights = (gate_weight[0], up_weight[0], down_weight[0])
    other_weights = tuple(lax.ppermute(w, "tp", CORE_SWAP) for w in own_weights)
    weights = (own_weights, other_weights)
    gain = norm_gain[0]
    rows = activations[0]
    for tick in range(TICKS):
        pieces = gathered(rms_normed(rows, gain), () if tick else other_weights[:2])
        shares, pair = scattered(feed_forward(pieces, weights))
        there = lax.ppermute(pair, ("section", "tp"), HOP_PAIR_SWAP)
        rows = plus(lax.ppermute(plus(rows, *shares), "section", HOP), there)
    return rows[None]


def solution(mesh):
    return jax.shard_map(
        per_device,
        mesh=mesh,
        in_specs=(
            P("section", "tp", None),
            P("section", None, "tp"),
            P("section", None, "tp"),
            P("section", "tp", None),
            P("section", None),
        ),
        out_specs=P("section", "tp", None),
        check_vma=False,
    )
```

```python
import jax
import jax.numpy as jnp
from jax import lax
from jax.sharding import PartitionSpec as P

TICKS = 2
N_SECTION = 8
N_Y, N_Z, N_CORE = 2, 8, 2
N_TP = N_Y * N_Z * N_CORE
FAR = N_Z // 2


def tp_index(y, z, core):
    return (y * N_Z + z % N_Z) * N_CORE + core


def tp_pairs(target):
    places = [(y, z, c) for y in range(N_Y) for z in range(N_Z) for c in range(N_CORE)]
    return [(tp_index(*place), tp_index(*target(*place))) for place in places]


Z_UP = tp_pairs(lambda y, z, c: (y, z + 1, c))
Z_DOWN = tp_pairs(lambda y, z, c: (y, z - 1, c))
Y_SWAP = tp_pairs(lambda y, z, c: (1 - y, z, c))
PAIR_SWAP = tp_pairs(lambda y, z, c: (1 - y, z + FAR, c))
CORE_SWAP = tp_pairs(lambda y, z, c: (y, z, 1 - c))
HOP = [(s, (s + 1) % N_SECTION) for s in range(N_SECTION)]
HOP_PAIR_SWAP = [(s * N_TP + a, t * N_TP + b) for s, t in HOP for a, b in PAIR_SWAP]


def up(block):
    return lax.ppermute(block, "tp", Z_UP)


def down(block):
    return lax.ppermute(block, "tp", Z_DOWN)


def rms_normed(rows, gain):
    wide = rows.astype(jnp.float32)
    scale = lax.rsqrt(jnp.mean(wide * wide, axis=1, keepdims=True) + 1e-05)
    return (wide * scale * gain[None, :]).astype(jnp.bfloat16)


def dot(a, b):
    return jnp.dot(a, b, preferred_element_type=jnp.float32)


def expand(normed, w_gate, w_up):
    gate = dot(normed, w_gate)
    up_part = dot(normed, w_up)
    return (jax.nn.silu(gate) * up_part).astype(jnp.bfloat16)


def plus(*terms):
    return sum(term.astype(jnp.float32) for term in terms).astype(jnp.bfloat16)


def stacked(*pieces):
    return jnp.concatenate(pieces, axis=0)


def gathered(own, after):
    count = own.shape[0]
    pieces = {("own", 0): own}
    pair = lax.ppermute(own, "tp", PAIR_SWAP)
    here = lax.ppermute(own, "tp", Y_SWAP)
    low, high = up(own), down(own)
    low, high, pair, here, *_ = lax.optimization_barrier((low, high, pair, here, *after))
    pieces["own", -1], pieces["own", 1], pieces["pair", FAR], pieces["pair", 0] = low, high, pair, here
    far = lax.ppermute(pair, "tp", Y_SWAP)
    low, high = up(stacked(low, pair, here)), down(stacked(high, pair, here))
    low, high, pieces["own", FAR] = lax.optimization_barrier((low, high, far))
    pieces["own", -2], pieces["pair", 3], pieces["pair", -1] = low[:count], low[count:2 * count], low[2 * count:]
    pieces["own", 2], pieces["pair", -3], pieces["pair", 1] = high[:count], high[count:2 * count], high[2 * count:]
    low, high = lax.optimization_barrier((up(low[:2 * count]), down(high[:2 * count])))
    pieces["own", -3], pieces["pair", 2] = low[:count], low[count:]
    pieces["own", 3], pieces["pair", -2] = high[:count], high[count:]
    return pieces


FIRST = tuple(("own", j) for j in (3, -3, FAR)) + tuple(("pair", j) for j in (2, -2, 1, -1, 0))
REST = tuple(("own", j) for j in (2, -2, 1, -1, 0)) + tuple(("pair", j) for j in (-3, 3, FAR))


def feed_forward(pieces, weights):
    count = pieces[FIRST[0]].shape[0]
    parts = {}
    for names in (FIRST, REST):
        rows = stacked(*(pieces[name] for name in names))
        units = lax.optimization_barrier([expand(rows, w_gate, w_up) for w_gate, w_up, _ in weights])
        part = sum(dot(u, w_down) for u, (_, _, w_down) in zip(units, weights)).astype(jnp.bfloat16)
        for i, name in enumerate(names):
            parts[name] = lax.optimization_barrier(part[i * count:(i + 1) * count])
    return parts


def scattered(parts):
    count = parts["own", 0].shape[0]
    near = stacked(*(parts[name] for name in (("pair", 1), ("pair", -1), ("own", FAR), ("pair", 0))))
    near = lax.ppermute(near, "tp", Y_SWAP)
    send_up = stacked(parts["own", 3], parts["pair", -2])
    send_down = stacked(parts["own", -3], parts["pair", 2])
    rise, fall = lax.optimization_barrier((up(send_up), down(send_down)))
    send_up = stacked(plus(parts["own", 2], rise[:count]), plus(parts["pair", -3], rise[count:]))
    send_down = stacked(plus(parts["own", -2], fall[:count]), plus(parts["pair", 3], fall[count:]))
    rise, fall = lax.optimization_barrier((up(send_up), down(send_down)))
    send_up = plus(parts["own", 1], rise[:count], near[:count])
    send_down = plus(parts["own", -1], fall[:count], near[count:2 * count])
    pair = plus(parts["pair", FAR], rise[count:], fall[count:], near[2 * count:3 * count])
    return (parts["own", 0], near[3 * count:], up(send_up), down(send_down)), pair


def per_device(activations, gate_weight, up_weight, down_weight, norm_gain):
    own_weights = (gate_weight[0], up_weight[0], down_weight[0])
    other_weights = tuple(lax.ppermute(w, "tp", CORE_SWAP) for w in own_weights)
    weights = (own_weights, other_weights)
    gain = norm_gain[0]
    rows = activations[0]
    for tick in range(TICKS):
        pieces = gathered(rms_normed(rows, gain), () if tick else other_weights[:2])
        shares, pair = scattered(feed_forward(pieces, weights))
        there = lax.ppermute(pair, ("section", "tp"), HOP_PAIR_SWAP)
        rows = plus(lax.ppermute(plus(rows, *shares), "section", HOP), there)
    return rows[None]


def solution(mesh):
    return jax.shard_map(
        per_device,
        mesh=mesh,
        in_specs=(
            P("section", "tp", None),
            P("section", None, "tp"),
            P("section", None, "tp"),
            P("section", "tp", None),
            P("section", None),
        ),
        out_specs=P("section", "tp", None),
        check_vma=False,
    )
```
